1024 devices in a mesh: expert: 16 (over x, core), replica: 64 (over y, z).
Axes of the slice: x: 8, y: 8, z: 8, core: 2. Of those that a mesh axis runs over, the one named last changes fastest.
Arguments:
- grad_out: bfloat16 [131072, 3584], P(('expert', 'replica')), may hold values from -6 to 6
- route_probs: bfloat16 [131072, 1], P(('expert', 'replica')), may hold values from 0.099609375 to 1
- routes: int32 [131072, 1], P(('expert', 'replica')), may hold values from 0 to 15; in each aligned block of 128 rows (0 to 127, 128 to 255, ...) at most 12 rows name the same one
- hidden_saved: bfloat16 [16, 64, 16, 12, 1024], P('expert', 'replica'), may hold values from -6 to 6
- weight_codes: bfloat16 [16, 1024, 3584], P('expert'), may hold values from -6 to 6, as said below
- weight_scales: int32 [16, 1024, 112], P('expert'), may hold values from 118 to 121
- subset_ids: int32 [16, 384], P('expert'), may hold values from 0 to 1023, as said below
Outputs:
- hidden_grad: bfloat16 [16, 64, 16, 12, 1024], P('expert', 'replica')
- weight_grad: float32 [16, 3584, 384], P('expert', 'replica')
- prob_grad: float32 [131072, 1], P(('expert', 'replica'))
The draws below stay inside these ranges and needn't reach their ends.
Inputs may be any that keep to these rules, and one draw needn't show every extreme that they name: Among the rows of one device no expert is named by more than 12 routes, and in some devices' rows an expert is named by exactly 12. `subset_ids`: each row holds 384 different hidden units. `weight_codes`: entries are of the four-bit code set: 0 and plus or minus 0.5, 1, 1.5, 2, 3, 4, 6.
All inputs are finite; a program needn't handle non-finite values.
Results may differ from the reference program's by a relative error of at most 0.0075.
Values may be sent and summed in bfloat16 or wider, within the bound.
No kernel may reach another device: no remote copies, remote signals or barrier semaphores. Data moves between devices by JAX's collectives and lax.ppermute only.
A program may use at most 64 MiB of HBM per device.

```python
import math
import jax
import jax.numpy as jnp
import numpy as np
from jax import lax

D = 3584
FF = 1024
SUB = 384
TOP = 1
TOK_DEV = 128
EXPERTS = 16
CAP = 12
TOKENS = 131072
N_EXPERT = 16
N_REPLICA = 64


def draw_weight_codes(key, part):
    key = jax.random.fold_in(key, 5)
    levels = jnp.array([0.0, 0.5, 1.0, 1.5, 2.0, 3.0, 4.0, 6.0, -0.5, -1.0, -1.5, -2.0, -3.0, -4.0, -6.0], jnp.float32)
    picks = jax.random.randint(key, (EXPERTS, FF, D), 0, 15)
    return levels[picks].astype(jnp.bfloat16)


def draw_subset_ids(key, part):
    key = jax.random.fold_in(key, 7)
    keys = jax.random.split(key, EXPERTS)

    def one_row(row_key):
        return jax.random.permutation(row_key, FF)[:SUB].astype(jnp.int32)
    return jax.vmap(one_row)(keys)


def place_ends(entries, stream_key, least, high):
    longest = entries.shape.index(max(entries.shape))
    spots = []
    for shift in (0, 1):
        where = [jax.random.randint(jax.random.fold_in(stream_key, axis), (), 0, length) for axis, length in enumerate(entries.shape)]
        where[longest] = (where[longest] + shift) % entries.shape[longest]
        spots.append(tuple(where))
    return entries.at[spots[0]].set(least).at[spots[1]].set(high)


def raised(entries, rng, source, target, shards_of, factor):
    def block_of(dim):
        return (jnp.arange(entries.shape[dim]) // (entries.shape[dim] // shards_of)).reshape((-1,) + (1,) * (entries.ndim - 1 - dim))

    one_side = jax.random.permutation(rng, shards_of)[block_of(target)]
    far = (block_of(target) + shards_of // 2) % shards_of
    return jnp.where((block_of(source) == one_side) | (block_of(source) == far), factor * entries, entries)


def block_scale(key, shape, cuts, low, largest):
    gain, own = 1.0, jax.random.fold_in(key, 6)
    for dim, shards_of in cuts:
        draws = jnp.exp(jax.random.uniform(jax.random.fold_in(own, dim), (shards_of,), jnp.float32, low / len(cuts), largest / len(cuts)))
        gain = gain * jnp.repeat(draws, shape[dim] // shards_of).reshape([-1 if axis == dim else 1 for axis in range(len(shape))])
    return gain


def shared_out(rng, own, number, rows, amount, top, limit, lean):
    order = jax.random.permutation(rng, amount)
    packed, ordinary = shares(amount, rows * top, limit, lean, True), shares(amount, rows * top, limit, lean, False)
    places = jnp.arange(amount)

    def named(tallies, turn):
        used = int((tallies > 0).sum())
        fixed = max(1, used // 4)
        moved = fixed + (places - fixed + turn * (used - fixed)) % max(1, amount - fixed)
        return jnp.zeros((amount,), jnp.int32).at[order[jnp.where(places < fixed, places, moved)]].set(jnp.asarray(tallies, jnp.int32))

    tallies = jnp.where(number % 4 == 0, named(packed, number // 4), named(ordinary, number - number // 4 - 1))
    mixed = jax.random.permutation(jax.random.fold_in(own, 3), amount)
    source_of, receiver = mixed[0:amount // 2 * 2:2], mixed[1:amount // 2 * 2:2]
    room = jnp.minimum(tallies[source_of] - 1, limit - tallies[receiver]) // 2
    room = jnp.where((source_of == order[0]) | (receiver == order[0]) | (tallies[receiver] == 0), 0, jnp.maximum(room, 0))
    moved = jax.random.randint(jax.random.fold_in(own, 4), (amount // 2,), 0, 1 << 20) % (room + 1)
    tallies = tallies.at[source_of].add(-moved).at[receiver].add(moved)
    members = jnp.searchsorted(jnp.cumsum(tallies), jnp.arange(rows * top), side="right").astype(jnp.int32)
    grid = members.reshape(top, rows).T
    grid = grid[jax.random.permutation(jax.random.fold_in(own, 1), rows)]
    turn = jax.random.randint(jax.random.fold_in(own, 2), (rows, 1), 0, top)
    return jnp.take_along_axis(grid, (jnp.arange(top)[None, :] + turn) % top, axis=1)


def shares(number_of, total, most, slope, full):
    weights = [(1 << 20) // math.isqrt(grade ** slope) + 1 for grade in range(1, number_of + 1)]
    largest = most if full else min(most, max(-(-total // number_of), total * weights[0] // sum(weights)))
    least = 1 if total - largest >= number_of - 1 else 0
    given, rest = [largest] + [least] * (number_of - 1), total - largest - least * (number_of - 1)
    while rest > 0:
        free = [i for i in range(1, number_of) if given[i] < largest] or [i for i in range(1, number_of) if given[i] < most]
        whole, budget = sum([weights[i] for i in free]), rest
        for i in free:
            more = min(most - given[i], max(1, budget * weights[i] // whole), rest)
            given[i] = given[i] + more
            rest = rest - more
    return np.array(given)


def gaussian(key, extent, scale, bound, pieces=(), kind=jnp.bfloat16):
    factor_of = block_scale(key, extent, pieces, -0.22, 0.18) if pieces else 1.0
    drawn = jax.random.normal(key, extent, jnp.float32) * scale * factor_of
    return jnp.minimum(jnp.maximum(drawn, -bound), bound).astype(kind)


def noise_with(own_key, shape, spread, limit, pieces, heavy, held_as=jnp.bfloat16):
    drawn = spread * jax.random.normal(own_key, shape, jnp.float32)
    if pieces:
        drawn = drawn * block_scale(own_key, shape, pieces, -0.22, 0.18)
    return jnp.clip(raised(drawn, jax.random.fold_in(own_key, 3), *heavy), -limit, limit).astype(held_as)


def setup_inputs(seed: int = 0) -> dict:
    arg_keys = jax.random.split(jax.random.key(seed), 8)
    grad_out = noise_with(arg_keys[0], (TOKENS, D), 0.25, 6.0, ((0, 1024),), (0, 1, 512, 6.0))
    route_probs = jnp.clip(0.099609375 + 0.9003906 * jax.random.uniform(arg_keys[1], (TOKENS, TOP), jnp.float32) ** block_scale(arg_keys[1], (TOKENS, TOP), ((0, 1024),), -0.2, 0.2), 0.099609375, 1.0).astype(jnp.bfloat16)
    routes_keys = jax.random.split(jax.random.fold_in(arg_keys[2], 1), TOKENS // TOK_DEV)
    routes_turns = jax.random.permutation(jax.random.fold_in(arg_keys[2], 3), TOKENS // TOK_DEV)
    routes = jax.vmap(lambda own, number: shared_out(jax.random.fold_in(arg_keys[2], 2), own, number, TOK_DEV, EXPERTS, TOP, CAP, 2))(routes_keys, routes_turns).reshape((TOKENS, TOP))
    hidden_saved = gaussian(arg_keys[3], (EXPERTS, N_REPLICA, N_EXPERT, CAP, FF), 1.0, 6.0, ((0, 16), (1, 64)))
    weight_codes = draw_weight_codes(jax.random.fold_in(arg_keys[7], 71), 0)
    weight_scales = place_ends(jax.random.randint(arg_keys[5], (EXPERTS, FF, D // 32), 118, 122), jax.random.fold_in(arg_keys[5], 1), 118, 121).astype(jnp.int32)
    subset_ids = draw_subset_ids(jax.random.fold_in(arg_keys[7], 71), 0)
    return {"grad_out": grad_out, "route_probs": route_probs, "routes": routes, "hidden_saved": hidden_saved, "weight_codes": weight_codes, "weight_scales": weight_scales, "subset_ids": subset_ids}


def dequantize(code_block, scale_block):
    scale_bf = jnp.exp2((scale_block - 127).astype(jnp.float32)).astype(jnp.bfloat16)
    shaped = code_block.reshape(FF, D // 32, 32) * scale_bf[:, :, None]
    return shaped.reshape(FF, D)


def reference(grad_out, route_probs, routes, hidden_saved, weight_codes, weight_scales, subset_ids):
    length = TOK_DEV * TOP
    flat_routes = routes.reshape(N_EXPERT, N_REPLICA, length)
    onehot = (flat_routes[..., None] == jnp.arange(EXPERTS, dtype=jnp.int32)).astype(jnp.int32)
    before = jnp.cumsum(onehot, axis=2) - onehot
    slot_index = jnp.sum(onehot * before, axis=3).astype(jnp.int32)
    source_grid = jnp.broadcast_to(jnp.arange(N_EXPERT, dtype=jnp.int32)[:, None, None], flat_routes.shape)
    replica_grid = jnp.broadcast_to(jnp.arange(N_REPLICA, dtype=jnp.int32)[None, :, None], flat_routes.shape)
    position = jnp.broadcast_to(jnp.arange(length, dtype=jnp.int32)[None, None, :], flat_routes.shape)
    slot_table = jnp.full((EXPERTS, N_REPLICA, N_EXPERT, CAP), length, jnp.int32)
    slot_table = slot_table.at[flat_routes, replica_grid, source_grid, slot_index].set(position)
    grad_blocks = grad_out.reshape(N_EXPERT, N_REPLICA, TOK_DEV, D)
    prob_blocks = route_probs.reshape(N_EXPERT, N_REPLICA, length)
    rep_axis = jnp.arange(N_REPLICA, dtype=jnp.int32)[:, None, None]
    src_axis = jnp.arange(N_EXPERT, dtype=jnp.int32)[None, :, None]

    def one_expert(expert_id):
        table_e = slot_table[expert_id]
        is_live = table_e < length
        clipped = jnp.minimum(table_e, length - 1)
        token_index = clipped // TOP
        rows_recv = grad_blocks[src_axis, rep_axis, token_index]
        rows_recv = jnp.where(is_live[..., None], rows_recv, jnp.zeros_like(rows_recv)).reshape(-1, D)
        weights_e = prob_blocks[src_axis, rep_axis, clipped]
        weights_e = jnp.where(is_live, weights_e, jnp.zeros_like(weights_e)).reshape(-1).astype(jnp.float32)
        weight = dequantize(weight_codes[expert_id], weight_scales[expert_id])
        hidden = hidden_saved[expert_id].reshape(-1, FF)
        through = lax.dot_general(rows_recv, weight, (((1,), (1,)), ((), ())), preferred_element_type=jnp.float32)
        grad_hidden = (weights_e[:, None] * through).astype(jnp.bfloat16)
        expert_out = jnp.dot(hidden, weight, preferred_element_type=jnp.float32).astype(jnp.bfloat16)
        scores = jnp.sum(rows_recv.astype(jnp.float32) * expert_out.astype(jnp.float32), axis=1)
        picked = jnp.take(hidden, subset_ids[expert_id], axis=1)
        scaled_hidden = (weights_e[:, None] * picked.astype(jnp.float32)).astype(jnp.bfloat16)
        grad_weight = lax.dot_general(rows_recv, scaled_hidden, (((0,), (0,)), ((), ())), preferred_element_type=jnp.float32)
        return (grad_hidden.reshape(N_REPLICA, N_EXPERT, CAP, FF), scores.reshape(N_REPLICA, N_EXPERT, CAP), grad_weight)

    hidden_grad, score_all, weight_grad = lax.map(one_expert, jnp.arange(EXPERTS, dtype=jnp.int32))
    prob_grad = score_all[flat_routes, replica_grid, source_grid, slot_index].reshape(TOKENS, TOP)
    return hidden_grad, weight_grad, prob_grad
```

```python
import functools

import jax
import jax.numpy as jnp
from jax import lax
from jax.experimental import pallas as pl
from jax.experimental.pallas import tpu as pltpu
from jax.sharding import PartitionSpec as P

F32 = jnp.float32
BF16 = jnp.bfloat16
BOTH = ("expert", "replica")
LIMIT = 48 * 1024 * 1024


def iota(shape, dim):
    return lax.broadcasted_iota(jnp.int32, shape, dim)


def ones_where(mask):
    return jnp.where(mask, 1.0, 0.0).astype(BF16)


def contract(a, b, da, db):
    return lax.dot_general(a, b, (((da,), (db,)), ((), ())), preferred_element_type=F32)


def slots_of(routes_row, experts_n):
    rows = routes_row.shape[1]
    named = iota((experts_n, rows), 0) == routes_row
    earlier = ones_where(iota((rows, rows), 0) < iota((rows, rows), 1))
    before = contract(ones_where(named), earlier, 1, 0)
    return named, jnp.sum(jnp.where(named, before, 0.0), axis=0, keepdims=True).astype(jnp.int32)


def pack_kernel(slots, experts_n, routes_ref, probs_ref, grad_ref, out_ref):
    routes = routes_ref[...]
    probs = probs_ref[...].astype(F32)
    rows = routes.shape[1]
    half = out_ref.shape[1]
    _, slot = slots_of(routes, experts_n)
    target = routes * (2 * slots) + slot
    places = iota((out_ref.shape[0], rows), 0)
    left = jnp.where(places == target, probs, 0.0).astype(BF16)
    right = jnp.where(places == target + slots, probs, 0.0).astype(BF16)
    place = jnp.concatenate([left, right], axis=1)
    step = 256
    for at in range(0, half, step):
        piece = jnp.concatenate(
            [grad_ref[:, at : at + step], grad_ref[:, half + at : half + at + step]], axis=0
        )
        out_ref[:, at : at + step] = contract(place, piece, 1, 0).astype(BF16)


def pick_kernel(ids_ref, hidden_ref, out_ref):
    chosen = ones_where(iota((hidden_ref.shape[1], ids_ref.shape[1]), 0) == ids_ref[...])
    out_ref[...] = contract(hidden_ref[...], chosen, 1, 0).astype(BF16)


def relay_kernel(slots, sources, side, parity_ref, rows_ref, out_ref, total):
    half = rows_ref.shape[1]
    width = 2 * half
    piece = width // (side * side)
    main = side * piece
    rows = rows_ref.shape[0]
    lane = iota((rows, 256), 1)
    place = jnp.where(lane < 128, lane, 128 + (lane & 63))
    slot, source = place >> 4, place & 15
    step = half // 2
    for at in range(0, width, step):
        pick = ones_where(
            iota((rows, 256), 0) == source * (2 * slots) + (at // half) * slots + slot
        )
        block = rows_ref[:, at % half : at % half + step]
        total[at : at + step, :] = contract(block, pick, 0, 0)
    low = iota((piece, 128), 1) < 64

    def spread(where):
        for to in range(side):
            for part in range(side):
                at = where(to, part) * piece
                out_ref[to, part * piece : (part + 1) * piece, :] = total[
                    at : at + piece, 0:128
                ].astype(BF16)
            for part in range(side // 2):
                one = where(to, part) * piece
                two = where(to, part + side // 2) * piece
                both = jnp.where(
                    low, total[one : one + piece, 128:256], total[two : two + piece, 128:256]
                )
                out_ref[to, main + part * piece : main + (part + 1) * piece, :] = both.astype(BF16)

    @pl.when(parity_ref[0] == 0)
    def _():
        spread(lambda to, part: to * side + part)

    @pl.when(parity_ref[0] == 1)
    def _():
        spread(lambda to, part: part * side + to)


def hidden_kernel(
    slots, sources, rows_ref, codes_ref, scales_ref, hidden_ref, out_ref, score_ref, total, factors
):
    step_n = pl.program_id(0)
    block = codes_ref.shape[1]
    halves = pl.num_programs(0) // 2
    groups = scales_ref.shape[0]
    places = hidden_ref.shape[0]

    @pl.when(step_n == 0)
    def _():
        factors[...] = jnp.exp2((scales_ref[...] - 127).astype(F32)).T.astype(BF16)
        total[...] = jnp.zeros_like(total)

    at = step_n * (block // 32) + (iota((groups, block), 1) >> 5)
    spread = contract(factors[...], ones_where(iota((groups, block), 0) == at), 1, 0)
    weight = codes_ref[...] * spread.astype(BF16)
    place = iota((places, rows_ref.shape[0]), 0)
    row = (place & 15) * (2 * slots) + (step_n // halves) * slots + (place >> 4)
    pick = ones_where(iota((places, rows_ref.shape[0]), 1) == row)
    rows = contract(pick, rows_ref[...], 1, 0).astype(BF16)
    total[...] += contract(rows, weight, 1, 1)

    @pl.when(step_n == pl.num_programs(0) - 1)
    def _():
        through = total[...]
        out_ref[...] = through.astype(BF16)
        score = jnp.sum(through * hidden_ref[...].astype(F32), axis=1, keepdims=True)
        by_slot = jnp.where(iota((places, 128), 1) == iota((places, 128), 0) >> 4, score, 0.0)
        by_source = jnp.where(
            iota((sources, places), 0) == iota((sources, places), 1) & 15, 1.0, 0.0
        )
        score_ref[...] = jnp.dot(
            by_source, by_slot, preferred_element_type=F32, precision=lax.Precision.HIGHEST
        )


def partial_kernel(side, me_ref, relayed_ref, *refs):
    picked, out_ref, total = refs[:-2], refs[-2], refs[-1]
    main = out_ref.shape[0]
    half = main // 2
    zeros = jnp.zeros((64, out_ref.shape[1]), BF16)
    total[...] = jnp.zeros_like(total)
    for distance in range(side):
        block = relayed_ref.at[lax.rem(me_ref[0] - distance + side, side)]
        own = picked[distance]
        total[...] += contract(block[:main, :], own[0:128, :], 1, 0)
        rest = own[128:192, :]
        tail = block[main : main + half, :]
        total[:half, :] += contract(tail, jnp.concatenate([rest, zeros], axis=0), 1, 0)
        total[half:, :] += contract(tail, jnp.concatenate([zeros, rest], axis=0), 1, 0)
    out_ref[...] = total[...].astype(BF16)


def prob_kernel(experts_n, routes_ref, probs_ref, returned_ref, out_ref):
    routes = routes_ref[...]
    named, slot = slots_of(routes, experts_n)
    mine = lax.dot_general(
        returned_ref[...],
        jnp.where(named, 1.0, 0.0),
        (((0,), (0,)), ((), ())),
        preferred_element_type=F32,
        precision=lax.Precision.HIGHEST,
    )
    score = jnp.sum(jnp.where(iota(mine.shape, 0) == slot, mine, 0.0), axis=0, keepdims=True)
    out_ref[...] = score / probs_ref[...].astype(F32)


VMEM = pl.BlockSpec(memory_space=pltpu.VMEM)
SMEM = pl.BlockSpec(memory_space=pltpu.SMEM)


def cost(flops, moved):
    return pl.CostEstimate(flops=flops, bytes_accessed=moved, transcendentals=0)


def per_device(
    side, grad_out, route_probs, routes, hidden_saved, weight_codes, weight_scales, subset_ids
):
    experts_n = lax.axis_size("expert")
    width = grad_out.shape[1]
    sources, slots, hidden_n = hidden_saved.shape[2:]
    subset = subset_ids.shape[1]
    places = sources * slots
    half = width // 2
    main = width // side
    replica = lax.axis_index("replica")
    parity = lax.axis_index("expert") % 2
    me = jnp.where(parity == 0, replica // side, replica % side).astype(jnp.int32)
    params = pltpu.CompilerParams(vmem_limit_bytes=LIMIT)

    def at(e, y, z):
        return e * side * side + (y % side) * side + z % side

    lines = [
        [[at(e, b, a) if e % 2 == turn else at(e, a, b) for b in range(side)] for e in range(experts_n) for a in range(side)]
        for turn in (0, 1)
    ]

    def moves(by):
        return [
            (at(e, y, z), at(e, y + by, z) if e % 2 == 0 else at(e, y, z + by))
            for e in range(experts_n)
            for y in range(side)
            for z in range(side)
        ]

    def exchange(x, turn):
        return lax.all_to_all(
            x, BOTH, split_axis=0, concat_axis=0, tiled=True, axis_index_groups=lines[turn]
        )

    routes_row = routes.reshape(1, -1)
    probs_row = route_probs.reshape(1, -1)
    hidden = hidden_saved.transpose(0, 1, 3, 2, 4).reshape(places, hidden_n)

    packed = pl.pallas_call(
        functools.partial(pack_kernel, slots, experts_n),
        out_shape=jax.ShapeDtypeStruct((2 * places, half), BF16),
        in_specs=[VMEM] * 3,
        out_specs=VMEM,
        compiler_params=params,
        cost_estimate=cost(8 * places * 128 * half, 3 * places * width),
    )(routes_row, probs_row, grad_out)
    received = lax.all_to_all(
        packed.reshape(experts_n, 2 * slots, half), "expert", split_axis=0, concat_axis=0, tiled=True
    ).reshape(2 * places, half)

    ids, _ = lax.optimization_barrier((subset_ids, packed))
    picked = pl.pallas_call(
        pick_kernel,
        out_shape=jax.ShapeDtypeStruct((places, subset), BF16),
        in_specs=[VMEM] * 2,
        out_specs=VMEM,
        compiler_params=params,
        cost_estimate=cost(2 * places * hidden_n * subset, 2 * places * hidden_n),
    )(ids, hidden)
    others = [lax.ppermute(picked, BOTH, moves(by)) for by in range(1, side)]
    received, others = lax.optimization_barrier((received, others))

    relay = pl.pallas_call(
        functools.partial(relay_kernel, slots, sources, side),
        out_shape=jax.ShapeDtypeStruct((side, main + main // 2, 128), BF16),
        in_specs=[SMEM, VMEM],
        out_specs=VMEM,
        scratch_shapes=[pltpu.VMEM((width, 256), F32)],
        compiler_params=params,
        cost_estimate=cost(8 * places * 256 * half, 4 * places * width),
    )(parity.reshape(1), received)
    relayed = exchange(relay, 0)

    blocks = 4
    hidden_grad, scores = pl.pallas_call(
        functools.partial(hidden_kernel, slots, sources),
        grid=(blocks,),
        out_shape=(
            jax.ShapeDtypeStruct((places, hidden_n), BF16),
            jax.ShapeDtypeStruct((sources, 128), F32),
        ),
        in_specs=[
            pl.BlockSpec((2 * places, width // blocks), lambda i: (0, i % (blocks // 2))),
            pl.BlockSpec((hidden_n, width // blocks), lambda i: (0, i)),
            pl.BlockSpec((width // 32, hidden_n), lambda i: (0, 0)),
            pl.BlockSpec((places, hidden_n), lambda i: (0, 0)),
        ],
        out_specs=(
            pl.BlockSpec((places, hidden_n), lambda i: (0, 0)),
            pl.BlockSpec((sources, 128), lambda i: (0, 0)),
        ),
        scratch_shapes=[
            pltpu.VMEM((places, hidden_n), F32),
            pltpu.VMEM((hidden_n, width // 32), BF16),
        ],
        compiler_params=params,
        cost_estimate=cost(4 * places * hidden_n * width, 2 * hidden_n * width),
    )(received, weight_codes[0], weight_scales[0].T, hidden)
    returned = lax.all_to_all(scores, "expert", split_axis=0, concat_axis=0, tiled=True)

    summed = pl.pallas_call(
        functools.partial(partial_kernel, side),
        out_shape=jax.ShapeDtypeStruct((main, subset), BF16),
        in_specs=[SMEM] + [VMEM] * (side + 1),
        out_specs=VMEM,
        scratch_shapes=[pltpu.VMEM((main, subset), F32)],
        compiler_params=params,
        cost_estimate=cost(2 * side * places * main * subset, 2 * side * places * (main + subset)),
    )(me.reshape(1), relayed, picked, *others)
    terms = exchange(summed.reshape(side, main // side, subset), 1)
    weight_grad = jnp.sum(terms.astype(F32), axis=0)

    prob_grad = pl.pallas_call(
        functools.partial(prob_kernel, experts_n),
        out_shape=jax.ShapeDtypeStruct(routes_row.shape, F32),
        in_specs=[VMEM] * 3,
        out_specs=VMEM,
        compiler_params=params,
    )(routes_row, probs_row, returned)
    return (
        hidden_grad.reshape(1, 1, slots, sources, hidden_n).transpose(0, 1, 3, 2, 4),
        weight_grad.reshape(1, main // side, subset),
        prob_grad.reshape(routes.shape),
    )


def solution(mesh):
    side = 8
    placed = (
        P(("expert", "replica"), None),
        P(("expert", "replica"), None),
        P(("expert", "replica"), None),
        P("expert", "replica", None, None, None),
        P("expert", None, None),
        P("expert", None, None),
        P("expert", None),
    )
    return jax.shard_map(
        functools.partial(per_device, side),
        mesh=mesh,
        in_specs=placed,
        out_specs=(
            P("expert", "replica", None, None, None),
            P("expert", "replica", None),
            P(("expert", "replica"), None),
        ),
        check_vma=False,
    )
```

```python
import functools

import jax
import jax.numpy as jnp
from jax import lax
from jax.experimental import pallas as pl
from jax.experimental.pallas import tpu as pltpu
from jax.sharding import PartitionSpec as P

F32 = jnp.float32
BF16 = jnp.bfloat16
BOTH = ("expert", "replica")
MIB = 1024 * 1024


def iota(shape, dim):
    return lax.broadcasted_iota(jnp.int32, shape, dim)


def ones_where(mask):
    return jnp.where(mask, 1.0, 0.0).astype(BF16)


def contract(a, b, da, db):
    return lax.dot_general(a, b, (((da,), (db,)), ((), ())), preferred_element_type=F32)


def slots_of(routes_row, experts_n):
    rows = routes_row.shape[1]
    named = iota((experts_n, rows), 0) == routes_row
    earlier = ones_where(iota((rows, rows), 0) < iota((rows, rows), 1))
    before = contract(ones_where(named), earlier, 1, 0)
    return named, jnp.sum(jnp.where(named, before, 0.0), axis=0, keepdims=True).astype(jnp.int32)


def pack_kernel(slots, experts_n, routes_ref, probs_ref, left_ref, right_ref, out_ref):
    routes = routes_ref[...]
    probs = probs_ref[...].astype(F32)
    _, slot = slots_of(routes, experts_n)
    target = routes * (2 * slots) + slot
    places = iota((out_ref.shape[0], routes.shape[1]), 0)
    left = jnp.where(places == target, probs, 0.0).astype(BF16)
    right = jnp.where(places == target + slots, probs, 0.0).astype(BF16)
    place = jnp.concatenate([left, right], axis=1)
    both = jnp.concatenate([left_ref[...], right_ref[...]], axis=0)
    out_ref[...] = contract(place, both, 1, 0).astype(BF16)


def pick_kernel(ids_ref, hidden_ref, out_ref):
    chosen = ones_where(iota((hidden_ref.shape[1], ids_ref.shape[1]), 0) == ids_ref[...])
    out_ref[...] = contract(hidden_ref[...], chosen, 1, 0).astype(BF16)


def relay_kernel(slots, sources, side, parity_ref, rows_ref, out_ref, total):
    half = rows_ref.shape[1]
    width = 2 * half
    piece = width // (side * side)
    main = side * piece
    rows = rows_ref.shape[0]
    lane = iota((rows, 256), 1)
    place = jnp.where(lane < 128, lane, 128 + (lane & 63))
    slot, source = place >> 4, place & 15
    step = half // 2
    for at in range(0, width, step):
        pick = ones_where(
            iota((rows, 256), 0) == source * (2 * slots) + (at // half) * slots + slot
        )
        block = rows_ref[:, at % half : at % half + step]
        total[at : at + step, :] = contract(block, pick, 0, 0)
    low = iota((piece, 128), 1) < 64

    def spread(where):
        for to in range(side):
            for part in range(side):
                at = where(to, part) * piece
                out_ref[to, part * piece : (part + 1) * piece, :] = total[
                    at : at + piece, 0:128
                ].astype(BF16)
            for part in range(side // 2):
                one = where(to, part) * piece
                two = where(to, part + side // 2) * piece
                both = jnp.where(
                    low, total[one : one + piece, 128:256], total[two : two + piece, 128:256]
                )
                out_ref[to, main + part * piece : main + (part + 1) * piece, :] = both.astype(BF16)

    @pl.when(parity_ref[0] == 0)
    def _():
        spread(lambda to, part: to * side + part)

    @pl.when(parity_ref[0] == 1)
    def _():
        spread(lambda to, part: part * side + to)


def weight_kernel(codes_ref, scales_ref, out_ref, factors):
    block = codes_ref.shape[1]
    groups = scales_ref.shape[0]
    step_n = pl.program_id(0)

    @pl.when(step_n == 0)
    def _():
        factors[...] = jnp.exp2((scales_ref[...] - 127).astype(F32)).T.astype(BF16)

    at = step_n * (block // 32) + (iota((groups, block), 1) >> 5)
    spread = contract(factors[...], ones_where(iota((groups, block), 0) == at), 1, 0)
    out_ref[...] = codes_ref[...] * spread.astype(BF16)


def hidden_kernel(slots, sources, me_ref, rows_hbm, weight_hbm, hidden_hbm, out_ref, *refs):
    score_refs, (rows_ref, weight_ref, hidden_ref, rows, sems) = refs[:-5], refs[-5:]
    radix = len(score_refs)
    places, hidden_n = out_ref.shape
    half = rows_ref.shape[1]
    blocks = sems.shape[0] - 2
    block = hidden_n // blocks
    loads = [pltpu.make_async_copy(rows_hbm, rows_ref, sems.at[blocks])]
    for n in range(blocks):
        part = pl.ds(n * block, block)
        loads.append(pltpu.make_async_copy(weight_hbm.at[part], weight_ref.at[part], sems.at[n]))
    loads.insert(2, pltpu.make_async_copy(hidden_hbm, hidden_ref, sems.at[blocks + 1]))
    for load in loads:
        load.start()
    rows_load, first_load, hidden_load, *rest = loads
    place = iota((places, rows_ref.shape[0]), 0)
    column = iota((places, rows_ref.shape[0]), 1)
    rows_load.wait()
    for part in range(2):
        pick = ones_where(column == (place & 15) * (2 * slots) + part * slots + (place >> 4))
        rows[:, part * half : (part + 1) * half] = contract(pick, rows_ref[...], 1, 0).astype(BF16)
    hidden_load.wait()
    score = jnp.zeros((places, 1), F32)
    for n, load in enumerate([first_load, *rest]):
        load.wait()
        part = slice(n * block, (n + 1) * block)
        through = contract(rows[...], weight_ref[part, :], 1, 1)
        out_ref[:, part] = through.astype(BF16)
        score += jnp.sum(through * hidden_ref[:, part].astype(F32), axis=1, keepdims=True)
    by_slot = jnp.where(iota((places, 128), 1) == iota((places, 128), 0) >> 4, score, 0.0)
    rows_n = sources // radix
    ahead = iota((rows_n, places), 0) * radix + me_ref[0]
    for low, score_ref in enumerate(score_refs):
        to = (ahead + low) & 15
        by_source = jnp.where(to == iota((rows_n, places), 1) & 15, 1.0, 0.0)
        score_ref[...] = jnp.dot(
            by_source, by_slot, preferred_element_type=F32, precision=lax.Precision.HIGHEST
        )


def partial_kernel(side, me_ref, relayed_ref, *refs):
    picked, out_ref, total = refs[:-2], refs[-2], refs[-1]
    main = out_ref.shape[0]
    half = main // 2
    zeros = jnp.zeros((64, out_ref.shape[1]), BF16)
    total[...] = jnp.zeros_like(total)
    for distance in range(side):
        block = relayed_ref.at[lax.rem(me_ref[0] - distance + side, side)]
        own = picked[distance]
        total[...] += contract(block[:main, :], own[0:128, :], 1, 0)
        rest = own[128:192, :]
        tail = block[main : main + half, :]
        total[:half, :] += contract(tail, jnp.concatenate([rest, zeros], axis=0), 1, 0)
        total[half:, :] += contract(tail, jnp.concatenate([zeros, rest], axis=0), 1, 0)
    out_ref[...] = total[...].astype(BF16)


def with_bit(count, bit, value):
    return [j for j in range(count) if (j >> bit) & 1 == value]


def regroup_kernel(bit, *refs):
    count = 2 * refs[0].shape[0]
    for value in range(2):
        rows = []
        for j in with_bit(count, bit + 1, value):
            held = (j >> bit) & 1
            row = with_bit(count, bit, held).index(j)
            rows.append(refs[held][row : row + 1, :])
        refs[2 + value][...] = jnp.concatenate(rows, axis=0)


def prob_kernel(experts_n, me_ref, routes_ref, probs_ref, *refs):
    returned_refs, out_ref = refs[:-1], refs[-1]
    routes = routes_ref[...]
    _, slot = slots_of(routes, experts_n)
    named = (me_ref[0] - iota((experts_n, routes.shape[1]), 0)) & (experts_n - 1)
    mine = lax.dot_general(
        jnp.concatenate([ref[...] for ref in returned_refs], axis=0),
        jnp.where(named == routes, 1.0, 0.0),
        (((0,), (0,)), ((), ())),
        preferred_element_type=F32,
        precision=lax.Precision.HIGHEST,
    )
    score = jnp.sum(jnp.where(iota(mine.shape, 0) == slot, mine, 0.0), axis=0, keepdims=True)
    out_ref[...] = score / probs_ref[...].astype(F32)


VMEM = pl.BlockSpec(memory_space=pltpu.VMEM)
SMEM = pl.BlockSpec(memory_space=pltpu.SMEM)
HBM = pl.BlockSpec(memory_space=pltpu.HBM)


def cost(flops, moved):
    return pl.CostEstimate(flops=flops, bytes_accessed=moved, transcendentals=0)


def per_device(
    side, grad_out, route_probs, routes, hidden_saved, weight_codes, weight_scales, subset_ids
):
    experts_n = lax.axis_size("expert")
    width = grad_out.shape[1]
    sources, slots, hidden_n = hidden_saved.shape[2:]
    subset = subset_ids.shape[1]
    places = sources * slots
    half = width // 2
    main = width // side
    replica = lax.axis_index("replica")
    expert = lax.axis_index("expert").reshape(1)
    parity = lax.axis_index("expert") % 2
    radix = 2
    me = jnp.where(parity == 0, replica // side, replica % side).astype(jnp.int32)
    params = pltpu.CompilerParams(vmem_limit_bytes=16 * MIB)
    streamed = pltpu.CompilerParams(vmem_limit_bytes=56 * MIB)

    def at(e, y, z):
        return e * side * side + (y % side) * side + z % side

    lines = [
        [[at(e, b, a) if e % 2 == turn else at(e, a, b) for b in range(side)] for e in range(experts_n) for a in range(side)]
        for turn in (0, 1)
    ]

    def moves(by):
        return [
            (at(e, y, z), at(e, y + by, z) if e % 2 == 0 else at(e, y, z + by))
            for e in range(experts_n)
            for y in range(side)
            for z in range(side)
        ]

    def exchange(x, turn):
        return lax.all_to_all(
            x, BOTH, split_axis=0, concat_axis=0, tiled=True, axis_index_groups=lines[turn]
        )

    def shifted(x, by):
        return lax.ppermute(x, "expert", [(e, (e + by) % experts_n) for e in range(experts_n)])

    routes_row = routes.reshape(1, -1)
    probs_row = route_probs.reshape(1, -1)
    hidden = hidden_saved.transpose(0, 1, 3, 2, 4).reshape(places, hidden_n)

    chunks = 2
    tokens = grad_out.shape[0]
    packed = pl.pallas_call(
        functools.partial(pack_kernel, slots, experts_n),
        grid=(chunks,),
        out_shape=jax.ShapeDtypeStruct((2 * places, half), BF16),
        in_specs=[
            pl.BlockSpec((1, tokens), lambda i: (0, 0)),
            pl.BlockSpec((1, tokens), lambda i: (0, 0)),
            pl.BlockSpec((tokens, half // chunks), lambda i: (0, i)),
            pl.BlockSpec((tokens, half // chunks), lambda i: (0, i + chunks)),
        ],
        out_specs=pl.BlockSpec((2 * places, half // chunks), lambda i: (0, i)),
        compiler_params=pltpu.CompilerParams(vmem_limit_bytes=63 * MIB),
        cost_estimate=cost(8 * places * 128 * half, 3 * places * width),
    )(routes_row, probs_row, grad_out, grad_out)
    received = lax.all_to_all(
        packed.reshape(experts_n, 2 * slots, half), "expert", split_axis=0, concat_axis=0, tiled=True
    ).reshape(2 * places, half)

    ids, scales, _ = lax.optimization_barrier((subset_ids, weight_scales[0].T, packed))
    picked = pl.pallas_call(
        pick_kernel,
        out_shape=jax.ShapeDtypeStruct((places, subset), BF16),
        in_specs=[VMEM] * 2,
        out_specs=VMEM,
        compiler_params=params,
        cost_estimate=cost(2 * places * hidden_n * subset, 2 * places * hidden_n),
    )(ids, hidden)
    others = [lax.ppermute(picked, BOTH, moves(by)) for by in range(1, side)]
    blocks = 4
    weight = pl.pallas_call(
        weight_kernel,
        grid=(blocks,),
        out_shape=jax.ShapeDtypeStruct((hidden_n, width), BF16),
        in_specs=[
            pl.BlockSpec((hidden_n, width // blocks), lambda i: (0, i)),
            pl.BlockSpec((width // 32, hidden_n), lambda i: (0, 0)),
        ],
        out_specs=pl.BlockSpec((hidden_n, width // blocks), lambda i: (0, i)),
        scratch_shapes=[pltpu.VMEM((hidden_n, width // 32), BF16)],
        compiler_params=streamed,
        cost_estimate=cost(256 * hidden_n * width, 4 * hidden_n * width),
    )(weight_codes[0], scales)
    received, others, weight = lax.optimization_barrier((received, others, weight))

    relay = pl.pallas_call(
        functools.partial(relay_kernel, slots, sources, side),
        out_shape=jax.ShapeDtypeStruct((side, main + main // 2, 128), BF16),
        in_specs=[SMEM, VMEM],
        out_specs=VMEM,
        scratch_shapes=[pltpu.VMEM((width, 256), F32)],
        compiler_params=params,
        cost_estimate=cost(8 * places * 256 * half, 4 * places * width),
    )(parity.reshape(1), received)
    relayed = exchange(relay, 0)

    hidden_grad, *scores = pl.pallas_call(
        functools.partial(hidden_kernel, slots, sources),
        out_shape=(
            jax.ShapeDtypeStruct((places, hidden_n), BF16),
            *[jax.ShapeDtypeStruct((sources // radix, 128), F32)] * radix,
        ),
        in_specs=[SMEM, HBM, HBM, HBM],
        out_specs=(VMEM,) + (VMEM,) * radix,
        scratch_shapes=[
            pltpu.VMEM((2 * places, half), BF16),
            pltpu.VMEM((hidden_n, width), BF16),
            pltpu.VMEM((places, hidden_n), BF16),
            pltpu.VMEM((places, width), BF16),
            pltpu.SemaphoreType.DMA((2 + 2,)),
        ],
        compiler_params=streamed,
        cost_estimate=cost(4 * places * hidden_n * width, 2 * hidden_n * width),
    )(expert, received, weight, hidden)

    def passed_on(bit, scores):
        return [scores[0], shifted(scores[1], 1 << bit)]

    def regrouped(bit, scores):
        return pl.pallas_call(
            functools.partial(regroup_kernel, bit),
            out_shape=[jax.ShapeDtypeStruct((sources // radix, 128), F32)] * 2,
            in_specs=[VMEM] * 2,
            out_specs=[VMEM] * 2,
            compiler_params=params,
        )(*scores)

    scores = regrouped(0, passed_on(0, scores))
    scores = regrouped(1, passed_on(1, scores))
    relayed, scores = lax.optimization_barrier((relayed, scores))
    scores = passed_on(2, scores)
    summed = pl.pallas_call(
        functools.partial(partial_kernel, side),
        out_shape=jax.ShapeDtypeStruct((main, subset), BF16),
        in_specs=[SMEM] + [VMEM] * (side + 1),
        out_specs=VMEM,
        scratch_shapes=[pltpu.VMEM((main, subset), F32)],
        compiler_params=params,
        cost_estimate=cost(2 * side * places * main * subset, 2 * side * places * (main + subset)),
    )(me.reshape(1), relayed, picked, *others)
    summed, scores = lax.optimization_barrier((summed, scores))
    returned = passed_on(3, regrouped(2, scores))
    terms = exchange(summed.reshape(side, main // side, subset), 1)
    weight_grad = jnp.sum(terms.astype(F32), axis=0)

    prob_grad = pl.pallas_call(
        functools.partial(prob_kernel, experts_n),
        out_shape=jax.ShapeDtypeStruct(routes_row.shape, F32),
        in_specs=[SMEM] + [VMEM] * (2 + radix),
        out_specs=VMEM,
        compiler_params=params,
    )(expert, routes_row, probs_row, *returned)
    return (
        hidden_grad.reshape(1, 1, slots, sources, hidden_n).transpose(0, 1, 3, 2, 4),
        weight_grad.reshape(1, main // side, subset),
        prob_grad.reshape(routes.shape),
    )


def solution(mesh):
    side = 8
    placed = (
        P(("expert", "replica"), None),
        P(("expert", "replica"), None),
        P(("expert", "replica"), None),
        P("expert", "replica", None, None, None),
        P("expert", None, None),
        P("expert", None, None),
        P("expert", None),
    )
    return jax.shard_map(
        functools.partial(per_device, side),
        mesh=mesh,
        in_specs=placed,
        out_specs=(
            P("expert", "replica", None, None, None),
            P("expert", "replica", None),
            P(("expert", "replica"), None),
        ),
        check_vma=False,
    )
```

```python
import functools

import jax
import jax.numpy as jnp
from jax import lax
from jax.experimental import pallas as pl
from jax.experimental.pallas import tpu as pltpu
from jax.sharding import PartitionSpec as P

F32 = jnp.float32
BF16 = jnp.bfloat16
BOTH = ("expert", "replica")
MIB = 1024 * 1024


def iota(shape, dim):
    return lax.broadcasted_iota(jnp.int32, shape, dim)


def ones_where(mask):
    return jnp.where(mask, 1.0, 0.0).astype(BF16)


def contract(a, b, da, db):
    return lax.dot_general(a, b, (((da,), (db,)), ((), ())), preferred_element_type=F32)


def slots_of(routes_row, experts_n):
    rows = routes_row.shape[1]
    named = iota((experts_n, rows), 0) == routes_row
    earlier = ones_where(iota((rows, rows), 0) < iota((rows, rows), 1))
    before = contract(ones_where(named), earlier, 1, 0)
    return named, jnp.sum(jnp.where(named, before, 0.0), axis=0, keepdims=True).astype(jnp.int32)


def pack_kernel(slots, experts_n, routes_ref, probs_ref, left_ref, right_ref, out_ref):
    routes = routes_ref[...]
    probs = probs_ref[...].astype(F32)
    _, slot = slots_of(routes, experts_n)
    target = routes * (2 * slots) + slot
    places = iota((out_ref.shape[0], routes.shape[1]), 0)
    left = jnp.where(places == target, probs, 0.0).astype(BF16)
    right = jnp.where(places == target + slots, probs, 0.0).astype(BF16)
    place = jnp.concatenate([left, right], axis=1)
    both = jnp.concatenate([left_ref[...], right_ref[...]], axis=0)
    out_ref[...] = contract(place, both, 1, 0).astype(BF16)


def pick_kernel(ids_ref, hidden_ref, out_ref):
    chosen = ones_where(iota((hidden_ref.shape[1], ids_ref.shape[1]), 0) == ids_ref[...])
    out_ref[...] = contract(hidden_ref[...], chosen, 1, 0).astype(BF16)


def relay_kernel(slots, sources, side, parity_ref, rows_ref, out_ref, total):
    half = rows_ref.shape[1]
    width = 2 * half
    piece = width // (side * side)
    main = side * piece
    rows = rows_ref.shape[0]
    lane = iota((rows, 256), 1)
    place = jnp.where(lane < 128, lane, 128 + (lane & 63))
    slot, source = place >> 4, place & 15
    step = half // 2
    for at in range(0, width, step):
        pick = ones_where(
            iota((rows, 256), 0) == source * (2 * slots) + (at // half) * slots + slot
        )
        block = rows_ref[:, at % half : at % half + step]
        total[at : at + step, :] = contract(block, pick, 0, 0)
    low = iota((piece, 128), 1) < 64

    def spread(where):
        for to in range(side):
            for part in range(side):
                at = where(to, part) * piece
                out_ref[to, part * piece : (part + 1) * piece, :] = total[
                    at : at + piece, 0:128
                ].astype(BF16)
            for part in range(side // 2):
                one = where(to, part) * piece
                two = where(to, part + side // 2) * piece
                both = jnp.where(
                    low, total[one : one + piece, 128:256], total[two : two + piece, 128:256]
                )
                out_ref[to, main + part * piece : main + (part + 1) * piece, :] = both.astype(BF16)

    @pl.when(parity_ref[0] == 0)
    def _():
        spread(lambda to, part: to * side + part)

    @pl.when(parity_ref[0] == 1)
    def _():
        spread(lambda to, part: part * side + to)


def weight_kernel(codes_ref, scales_ref, out_ref, factors):
    block = codes_ref.shape[1]
    groups = scales_ref.shape[0]
    step_n = pl.program_id(0)

    @pl.when(step_n == 0)
    def _():
        factors[...] = jnp.exp2((scales_ref[...] - 127).astype(F32)).T.astype(BF16)

    at = step_n * (block // 32) + (iota((groups, block), 1) >> 5)
    spread = contract(factors[...], ones_where(iota((groups, block), 0) == at), 1, 0)
    out_ref[...] = codes_ref[...] * spread.astype(BF16)


def hidden_kernel(slots, sources, me_ref, rows_hbm, weight_hbm, hidden_hbm, out_ref, *refs):
    score_refs, (rows_ref, weight_ref, hidden_ref, rows, sems) = refs[:-5], refs[-5:]
    radix = len(score_refs)
    places, hidden_n = out_ref.shape
    half = rows_ref.shape[1]
    blocks = sems.shape[0] - 2
    block = hidden_n // blocks
    loads = [pltpu.make_async_copy(rows_hbm, rows_ref, sems.at[blocks])]
    for n in range(blocks):
        part = pl.ds(n * block, block)
        loads.append(pltpu.make_async_copy(weight_hbm.at[part], weight_ref.at[part], sems.at[n]))
    loads.insert(2, pltpu.make_async_copy(hidden_hbm, hidden_ref, sems.at[blocks + 1]))
    for load in loads:
        load.start()
    rows_load, first_load, hidden_load, *rest = loads
    place = iota((places, rows_ref.shape[0]), 0)
    column = iota((places, rows_ref.shape[0]), 1)
    rows_load.wait()
    for part in range(2):
        pick = ones_where(column == (place & 15) * (2 * slots) + part * slots + (place >> 4))
        rows[:, part * half : (part + 1) * half] = contract(pick, rows_ref[...], 1, 0).astype(BF16)
    hidden_load.wait()
    score = jnp.zeros((places, 1), F32)
    for n, load in enumerate([first_load, *rest]):
        load.wait()
        part = slice(n * block, (n + 1) * block)
        through = contract(rows[...], weight_ref[part, :], 1, 1)
        out_ref[:, part] = through.astype(BF16)
        score += jnp.sum(through * hidden_ref[:, part].astype(F32), axis=1, keepdims=True)
    by_slot = jnp.where(iota((places, 128), 1) == iota((places, 128), 0) >> 4, score, 0.0)
    rows_n = sources // radix
    ahead = iota((rows_n, places), 0) * radix + me_ref[0]
    for low, score_ref in enumerate(score_refs):
        to = (ahead + low) & 15
        by_source = jnp.where(to == iota((rows_n, places), 1) & 15, 1.0, 0.0)
        score_ref[...] = jnp.dot(
            by_source, by_slot, preferred_element_type=F32, precision=lax.Precision.HIGHEST
        )


def partial_kernel(side, me_ref, relayed_ref, *refs):
    picked, out_ref, total = refs[:-2], refs[-2], refs[-1]
    main = out_ref.shape[0]
    half = main // 2
    zeros = jnp.zeros((64, out_ref.shape[1]), BF16)
    total[...] = jnp.zeros_like(total)
    for distance in range(side):
        block = relayed_ref.at[lax.rem(me_ref[0] - distance + side, side)]
        own = picked[distance]
        total[...] += contract(block[:main, :], own[0:128, :], 1, 0)
        rest = own[128:192, :]
        tail = block[main : main + half, :]
        total[:half, :] += contract(tail, jnp.concatenate([rest, zeros], axis=0), 1, 0)
        total[half:, :] += contract(tail, jnp.concatenate([zeros, rest], axis=0), 1, 0)
    out_ref[...] = total[...].astype(BF16)


def with_bit(count, bit, value):
    return [j for j in range(count) if (j >> bit) & 1 == value]


def regroup_kernel(bit, *refs):
    count = 2 * refs[0].shape[0]
    for value in range(2):
        rows = []
        for j in with_bit(count, bit + 1, value):
            held = (j >> bit) & 1
            row = with_bit(count, bit, held).index(j)
            rows.append(refs[held][row : row + 1, :])
        refs[2 + value][...] = jnp.concatenate(rows, axis=0)


def prob_kernel(experts_n, me_ref, routes_ref, probs_ref, *refs):
    returned_refs, out_ref = refs[:-1], refs[-1]
    routes = routes_ref[...]
    _, slot = slots_of(routes, experts_n)
    named = (me_ref[0] - iota((experts_n, routes.shape[1]), 0)) & (experts_n - 1)
    mine = lax.dot_general(
        jnp.concatenate([ref[...] for ref in returned_refs], axis=0),
        jnp.where(named == routes, 1.0, 0.0),
        (((0,), (0,)), ((), ())),
        preferred_element_type=F32,
        precision=lax.Precision.HIGHEST,
    )
    score = jnp.sum(jnp.where(iota(mine.shape, 0) == slot, mine, 0.0), axis=0, keepdims=True)
    out_ref[...] = score / probs_ref[...].astype(F32)


VMEM = pl.BlockSpec(memory_space=pltpu.VMEM)
SMEM = pl.BlockSpec(memory_space=pltpu.SMEM)
HBM = pl.BlockSpec(memory_space=pltpu.HBM)


def cost(flops, moved):
    return pl.CostEstimate(flops=flops, bytes_accessed=moved, transcendentals=0)


def per_device(
    side, grad_out, route_probs, routes, hidden_saved, weight_codes, weight_scales, subset_ids
):
    experts_n = lax.axis_size("expert")
    width = grad_out.shape[1]
    sources, slots, hidden_n = hidden_saved.shape[2:]
    subset = subset_ids.shape[1]
    places = sources * slots
    half = width // 2
    main = width // side
    replica = lax.axis_index("replica")
    expert = lax.axis_index("expert").reshape(1)
    parity = lax.axis_index("expert") % 2
    radix = 2
    me = jnp.where(parity == 0, replica // side, replica % side).astype(jnp.int32)
    params = pltpu.CompilerParams(vmem_limit_bytes=16 * MIB)
    streamed = pltpu.CompilerParams(vmem_limit_bytes=56 * MIB)

    def at(e, y, z):
        return e * side * side + (y % side) * side + z % side

    lines = [
        [[at(e, b, a) if e % 2 == turn else at(e, a, b) for b in range(side)] for e in range(experts_n) for a in range(side)]
        for turn in (0, 1)
    ]

    def moves(by):
        return [
            (at(e, y, z), at(e, y + by, z) if e % 2 == 0 else at(e, y, z + by))
            for e in range(experts_n)
            for y in range(side)
            for z in range(side)
        ]

    def exchange(x, turn):
        return lax.all_to_all(
            x, BOTH, split_axis=0, concat_axis=0, tiled=True, axis_index_groups=lines[turn]
        )

    def shifted(x, by):
        return lax.ppermute(x, "expert", [(e, (e + by) % experts_n) for e in range(experts_n)])

    routes_row = routes.reshape(1, -1)
    probs_row = route_probs.reshape(1, -1)
    hidden = hidden_saved.transpose(0, 1, 3, 2, 4).reshape(places, hidden_n)

    chunks = 2
    tokens = grad_out.shape[0]
    packed = pl.pallas_call(
        functools.partial(pack_kernel, slots, experts_n),
        grid=(chunks,),
        out_shape=jax.ShapeDtypeStruct((2 * places, half), BF16),
        in_specs=[
            pl.BlockSpec((1, tokens), lambda i: (0, 0)),
            pl.BlockSpec((1, tokens), lambda i: (0, 0)),
            pl.BlockSpec((tokens, half // chunks), lambda i: (0, i)),
            pl.BlockSpec((tokens, half // chunks), lambda i: (0, i + chunks)),
        ],
        out_specs=pl.BlockSpec((2 * places, half // chunks), lambda i: (0, i)),
        compiler_params=pltpu.CompilerParams(vmem_limit_bytes=63 * MIB),
        cost_estimate=cost(8 * places * 128 * half, 3 * places * width),
    )(routes_row, probs_row, grad_out, grad_out)
    received = lax.all_to_all(
        packed.reshape(experts_n, 2 * slots, half), "expert", split_axis=0, concat_axis=0, tiled=True
    ).reshape(2 * places, half)

    ids, scales, _ = lax.optimization_barrier((subset_ids, weight_scales[0].T, packed))
    picked = pl.pallas_call(
        pick_kernel,
        out_shape=jax.ShapeDtypeStruct((places, subset), BF16),
        in_specs=[VMEM] * 2,
        out_specs=VMEM,
        compiler_params=params,
        cost_estimate=cost(2 * places * hidden_n * subset, 2 * places * hidden_n),
    )(ids, hidden)
    others = [lax.ppermute(picked, BOTH, moves(by)) for by in range(1, side)]
    blocks = 4
    weight = pl.pallas_call(
        weight_kernel,
        grid=(blocks,),
        out_shape=jax.ShapeDtypeStruct((hidden_n, width), BF16),
        in_specs=[
            pl.BlockSpec((hidden_n, width // blocks), lambda i: (0, i)),
            pl.BlockSpec((width // 32, hidden_n), lambda i: (0, 0)),
        ],
        out_specs=pl.BlockSpec((hidden_n, width // blocks), lambda i: (0, i)),
        scratch_shapes=[pltpu.VMEM((hidden_n, width // 32), BF16)],
        compiler_params=streamed,
        cost_estimate=cost(256 * hidden_n * width, 4 * hidden_n * width),
    )(weight_codes[0], scales)
    received, others, weight = lax.optimization_barrier((received, others, weight))

    relay = pl.pallas_call(
        functools.partial(relay_kernel, slots, sources, side),
        out_shape=jax.ShapeDtypeStruct((side, main + main // 2, 128), BF16),
        in_specs=[SMEM, VMEM],
        out_specs=VMEM,
        scratch_shapes=[pltpu.VMEM((width, 256), F32)],
        compiler_params=params,
        cost_estimate=cost(8 * places * 256 * half, 4 * places * width),
    )(parity.reshape(1), received)
    relayed = exchange(relay, 0)

    hidden_grad, *scores = pl.pallas_call(
        functools.partial(hidden_kernel, slots, sources),
        out_shape=(
            jax.ShapeDtypeStruct((places, hidden_n), BF16),
            *[jax.ShapeDtypeStruct((sources // radix, 128), F32)] * radix,
        ),
        in_specs=[SMEM, HBM, HBM, HBM],
        out_specs=(VMEM,) + (VMEM,) * radix,
        scratch_shapes=[
            pltpu.VMEM((2 * places, half), BF16),
            pltpu.VMEM((hidden_n, width), BF16),
            pltpu.VMEM((places, hidden_n), BF16),
            pltpu.VMEM((places, width), BF16),
            pltpu.SemaphoreType.DMA((2 + 2,)),
        ],
        compiler_params=streamed,
        cost_estimate=cost(4 * places * hidden_n * width, 2 * hidden_n * width),
    )(expert, received, weight, hidden)

    def passed_on(bit, scores):
        return [scores[0], shifted(scores[1], 1 << bit)]

    def regrouped(bit, scores):
        return pl.pallas_call(
            functools.partial(regroup_kernel, bit),
            out_shape=[jax.ShapeDtypeStruct((sources // radix, 128), F32)] * 2,
            in_specs=[VMEM] * 2,
            out_specs=[VMEM] * 2,
            compiler_params=params,
        )(*scores)

    scores = regrouped(0, passed_on(0, scores))
    scores = regrouped(1, passed_on(1, scores))
    scores = passed_on(2, scores)
    summed = pl.pallas_call(
        functools.partial(partial_kernel, side),
        out_shape=jax.ShapeDtypeStruct((main, subset), BF16),
        in_specs=[SMEM] + [VMEM] * (side + 1),
        out_specs=VMEM,
        scratch_shapes=[pltpu.VMEM((main, subset), F32)],
        compiler_params=params,
        cost_estimate=cost(2 * side * places * main * subset, 2 * side * places * (main + subset)),
    )(me.reshape(1), relayed, picked, *others)
    summed, scores = lax.optimization_barrier((summed, scores))
    returned = passed_on(3, regrouped(2, scores))
    terms = exchange(summed.reshape(side, main // side, subset), 1)
    weight_grad = jnp.sum(terms.astype(F32), axis=0)

    prob_grad = pl.pallas_call(
        functools.partial(prob_kernel, experts_n),
        out_shape=jax.ShapeDtypeStruct(routes_row.shape, F32),
        in_specs=[SMEM] + [VMEM] * (2 + radix),
        out_specs=VMEM,
        compiler_params=params,
    )(expert, routes_row, probs_row, *returned)
    return (
        hidden_grad.reshape(1, 1, slots, sources, hidden_n).transpose(0, 1, 3, 2, 4),
        weight_grad.reshape(1, main // side, subset),
        prob_grad.reshape(routes.shape),
    )


def solution(mesh):
    side = 8
    placed = (
        P(("expert", "replica"), None),
        P(("expert", "replica"), None),
        P(("expert", "replica"), None),
        P("expert", "replica", None, None, None),
        P("expert", None, None),
        P("expert", None, None),
        P("expert", None),
    )
    return jax.shard_map(
        functools.partial(per_device, side),
        mesh=mesh,
        in_specs=placed,
        out_specs=(
            P("expert", "replica", None, None, None),
            P("expert", "replica", None),
            P(("expert", "replica"), None),
        ),
        check_vma=False,
    )
```

```python
import functools

import jax
import jax.numpy as jnp
from jax import lax
from jax.experimental import pallas as pl
from jax.experimental.pallas import tpu as pltpu
from jax.sharding import PartitionSpec as P

F32 = jnp.float32
BF16 = jnp.bfloat16
F8 = jnp.float8_e5m2
BOTH = ("expert", "replica")
MIB = 1024 * 1024


def iota(shape, dim):
    return lax.broadcasted_iota(jnp.int32, shape, dim)


def ones_where(mask):
    return jnp.where(mask, 1.0, 0.0).astype(BF16)


def contract(a, b, da, db):
    return lax.dot_general(a, b, (((da,), (db,)), ((), ())), preferred_element_type=F32)


def slots_of(routes_row, experts_n):
    rows = routes_row.shape[1]
    named = iota((experts_n, rows), 0) == routes_row
    earlier = ones_where(iota((rows, rows), 0) < iota((rows, rows), 1))
    before = contract(ones_where(named), earlier, 1, 0)
    return named, jnp.sum(jnp.where(named, before, 0.0), axis=0, keepdims=True).astype(jnp.int32)


def pack_kernel(slots, experts_n, routes_ref, probs_ref, left_ref, right_ref, out_ref):
    routes = routes_ref[...]
    probs = probs_ref[...].astype(F32)
    _, slot = slots_of(routes, experts_n)
    target = routes * (2 * slots) + slot
    places = iota((out_ref.shape[0], routes.shape[1]), 0)
    left = jnp.where(places == target, probs, 0.0).astype(BF16)
    right = jnp.where(places == target + slots, probs, 0.0).astype(BF16)
    place = jnp.concatenate([left, right], axis=1)
    both = jnp.concatenate([left_ref[...], right_ref[...]], axis=0)
    out_ref[...] = contract(place, both, 1, 0).astype(BF16)


def pick_kernel(ids_ref, hidden_ref, out_ref):
    chosen = ones_where(iota((hidden_ref.shape[1], ids_ref.shape[1]), 0) == ids_ref[...])
    out_ref[...] = contract(hidden_ref[...], chosen, 1, 0).astype(BF16)


def relay_kernel(slots, sources, side, parity_ref, rows_ref, out_ref, total):
    half = rows_ref.shape[1]
    width = 2 * half
    piece = width // (side * side)
    main = side * piece
    rows = rows_ref.shape[0]
    lane = iota((rows, 256), 1)
    place = jnp.where(lane < 128, lane, 128 + (lane & 63))
    slot, source = place >> 4, place & 15
    step = half // 2
    for at in range(0, width, step):
        pick = ones_where(
            iota((rows, 256), 0) == source * (2 * slots) + (at // half) * slots + slot
        )
        block = rows_ref[:, at % half : at % half + step]
        total[at : at + step, :] = contract(block, pick, 0, 0)
    low = iota((piece, 128), 1) < 64

    def spread(where):
        for to in range(side):
            for part in range(side):
                at = where(to, part) * piece
                out_ref[to, part * piece : (part + 1) * piece, :] = total[
                    at : at + piece, 0:128
                ].astype(BF16)
            for part in range(side // 2):
                one = where(to, part) * piece
                two = where(to, part + side // 2) * piece
                both = jnp.where(
                    low, total[one : one + piece, 128:256], total[two : two + piece, 128:256]
                )
                out_ref[to, main + part * piece : main + (part + 1) * piece, :] = both.astype(BF16)

    @pl.when(parity_ref[0] == 0)
    def _():
        spread(lambda to, part: to * side + part)

    @pl.when(parity_ref[0] == 1)
    def _():
        spread(lambda to, part: part * side + to)


def weight_kernel(codes_ref, scales_ref, out_ref, factors):
    block = codes_ref.shape[1]
    groups = scales_ref.shape[0]
    step_n = pl.program_id(0)

    @pl.when(step_n == 0)
    def _():
        factors[...] = jnp.exp2((scales_ref[...] - 127).astype(F32)).T.astype(BF16)

    at = step_n * (block // 32) + (iota((groups, block), 1) >> 5)
    spread = contract(factors[...], ones_where(iota((groups, block), 0) == at), 1, 0)
    out_ref[...] = (codes_ref[...] * spread.astype(BF16)).astype(out_ref.dtype)


def hidden_kernel(slots, sources, me_ref, rows_hbm, weight_hbm, hidden_hbm, out_ref, *refs):
    score_refs, (rows_ref, weight_ref, hidden_ref, rows, sems) = refs[:-5], refs[-5:]
    radix = len(score_refs)
    places, hidden_n = out_ref.shape
    half = rows_ref.shape[1]
    blocks = sems.shape[0] - 2
    block = hidden_n // blocks
    loads = [pltpu.make_async_copy(rows_hbm, rows_ref, sems.at[blocks])]
    for n in range(blocks):
        part = pl.ds(n * block, block)
        loads.append(pltpu.make_async_copy(weight_hbm.at[part], weight_ref.at[part], sems.at[n]))
    loads.insert(2, pltpu.make_async_copy(hidden_hbm, hidden_ref, sems.at[blocks + 1]))
    for load in loads:
        load.start()
    rows_load, first_load, hidden_load, *rest = loads
    place = iota((places, rows_ref.shape[0]), 0)
    column = iota((places, rows_ref.shape[0]), 1)
    rows_load.wait()
    for part in range(2):
        pick = ones_where(column == (place & 15) * (2 * slots) + part * slots + (place >> 4))
        rows[:, part * half : (part + 1) * half] = contract(pick, rows_ref[...], 1, 0).astype(BF16)
    hidden_load.wait()
    score = jnp.zeros((places, 1), F32)
    for n, load in enumerate([first_load, *rest]):
        load.wait()
        part = slice(n * block, (n + 1) * block)
        through = contract(rows[...], weight_ref[part, :].astype(BF16), 1, 1)
        out_ref[:, part] = through.astype(BF16)
        score += jnp.sum(through * hidden_ref[:, part].astype(F32), axis=1, keepdims=True)
    by_slot = jnp.where(iota((places, 128), 1) == iota((places, 128), 0) >> 4, score, 0.0)
    rows_n = sources // radix
    ahead = iota((rows_n, places), 0) * radix + me_ref[0]
    for low, score_ref in enumerate(score_refs):
        to = (ahead + low) & 15
        by_source = jnp.where(to == iota((rows_n, places), 1) & 15, 1.0, 0.0)
        score_ref[...] = jnp.dot(
            by_source, by_slot, preferred_element_type=F32, precision=lax.Precision.HIGHEST
        )


def partial_kernel(side, me_ref, relayed_ref, *refs):
    picked, out_ref, total = refs[:-2], refs[-2], refs[-1]
    main = out_ref.shape[0]
    half = main // 2
    zeros = jnp.zeros((64, out_ref.shape[1]), BF16)
    total[...] = jnp.zeros_like(total)
    for distance in range(side):
        block = relayed_ref.at[lax.rem(me_ref[0] - distance + side, side)]
        own = picked[distance]
        total[...] += contract(block[:main, :], own[0:128, :], 1, 0)
        rest = own[128:192, :]
        tail = block[main : main + half, :]
        total[:half, :] += contract(tail, jnp.concatenate([rest, zeros], axis=0), 1, 0)
        total[half:, :] += contract(tail, jnp.concatenate([zeros, rest], axis=0), 1, 0)
    out_ref[...] = total[...].astype(BF16)


def with_bit(count, bit, value):
    return [j for j in range(count) if (j >> bit) & 1 == value]


def regroup_kernel(bit, *refs):
    count = 2 * refs[0].shape[0]
    for value in range(2):
        rows = []
        for j in with_bit(count, bit + 1, value):
            held = (j >> bit) & 1
            row = with_bit(count, bit, held).index(j)
            rows.append(refs[held][row : row + 1, :])
        refs[2 + value][...] = jnp.concatenate(rows, axis=0)


def prob_kernel(experts_n, me_ref, routes_ref, probs_ref, *refs):
    returned_refs, out_ref = refs[:-1], refs[-1]
    routes = routes_ref[...]
    _, slot = slots_of(routes, experts_n)
    named = (me_ref[0] - iota((experts_n, routes.shape[1]), 0)) & (experts_n - 1)
    mine = lax.dot_general(
        jnp.concatenate([ref[...] for ref in returned_refs], axis=0),
        jnp.where(named == routes, 1.0, 0.0),
        (((0,), (0,)), ((), ())),
        preferred_element_type=F32,
        precision=lax.Precision.HIGHEST,
    )
    score = jnp.sum(jnp.where(iota(mine.shape, 0) == slot, mine, 0.0), axis=0, keepdims=True)
    out_ref[...] = score / probs_ref[...].astype(F32)


VMEM = pl.BlockSpec(memory_space=pltpu.VMEM)
SMEM = pl.BlockSpec(memory_space=pltpu.SMEM)
HBM = pl.BlockSpec(memory_space=pltpu.HBM)


def cost(flops, moved):
    return pl.CostEstimate(flops=flops, bytes_accessed=moved, transcendentals=0)


def per_device(
    side, grad_out, route_probs, routes, hidden_saved, weight_codes, weight_scales, subset_ids
):
    experts_n = lax.axis_size("expert")
    width = grad_out.shape[1]
    sources, slots, hidden_n = hidden_saved.shape[2:]
    subset = subset_ids.shape[1]
    places = sources * slots
    half = width // 2
    main = width // side
    replica = lax.axis_index("replica")
    expert = lax.axis_index("expert").reshape(1)
    parity = lax.axis_index("expert") % 2
    radix = 2
    me = jnp.where(parity == 0, replica // side, replica % side).astype(jnp.int32)
    params = pltpu.CompilerParams(vmem_limit_bytes=16 * MIB)
    streamed = pltpu.CompilerParams(vmem_limit_bytes=56 * MIB)

    def at(e, y, z):
        return e * side * side + (y % side) * side + z % side

    lines = [
        [[at(e, b, a) if e % 2 == turn else at(e, a, b) for b in range(side)] for e in range(experts_n) for a in range(side)]
        for turn in (0, 1)
    ]

    def moves(by):
        return [
            (at(e, y, z), at(e, y + by, z) if e % 2 == 0 else at(e, y, z + by))
            for e in range(experts_n)
            for y in range(side)
            for z in range(side)
        ]

    def exchange(x, turn):
        return lax.all_to_all(
            x, BOTH, split_axis=0, concat_axis=0, tiled=True, axis_index_groups=lines[turn]
        )

    def shifted(x, by):
        return lax.ppermute(x, "expert", [(e, (e + by) % experts_n) for e in range(experts_n)])

    routes_row = routes.reshape(1, -1)
    probs_row = route_probs.reshape(1, -1)
    hidden = hidden_saved.transpose(0, 1, 3, 2, 4).reshape(places, hidden_n)

    chunks = 2
    tokens = grad_out.shape[0]
    packed = pl.pallas_call(
        functools.partial(pack_kernel, slots, experts_n),
        grid=(chunks,),
        out_shape=jax.ShapeDtypeStruct((2 * places, half), BF16),
        in_specs=[
            pl.BlockSpec((1, tokens), lambda i: (0, 0)),
            pl.BlockSpec((1, tokens), lambda i: (0, 0)),
            pl.BlockSpec((tokens, half // chunks), lambda i: (0, i)),
            pl.BlockSpec((tokens, half // chunks), lambda i: (0, i + chunks)),
        ],
        out_specs=pl.BlockSpec((2 * places, half // chunks), lambda i: (0, i)),
        compiler_params=pltpu.CompilerParams(vmem_limit_bytes=63 * MIB),
        cost_estimate=cost(8 * places * 128 * half, 3 * places * width),
    )(routes_row, probs_row, grad_out, grad_out)
    received = lax.all_to_all(
        packed.reshape(experts_n, 2 * slots, half), "expert", split_axis=0, concat_axis=0, tiled=True
    ).reshape(2 * places, half)

    ids, scales, _ = lax.optimization_barrier((subset_ids, weight_scales[0].T, packed))
    picked = pl.pallas_call(
        pick_kernel,
        out_shape=jax.ShapeDtypeStruct((places, subset), BF16),
        in_specs=[VMEM] * 2,
        out_specs=VMEM,
        compiler_params=params,
        cost_estimate=cost(2 * places * hidden_n * subset, 2 * places * hidden_n),
    )(ids, hidden)
    others = [lax.ppermute(picked, BOTH, moves(by)) for by in range(1, side)]
    blocks = 4
    weight = pl.pallas_call(
        weight_kernel,
        grid=(blocks,),
        out_shape=jax.ShapeDtypeStruct((hidden_n, width), F8),
        in_specs=[
            pl.BlockSpec((hidden_n, width // blocks), lambda i: (0, i)),
            pl.BlockSpec((width // 32, hidden_n), lambda i: (0, 0)),
        ],
        out_specs=pl.BlockSpec((hidden_n, width // blocks), lambda i: (0, i)),
        scratch_shapes=[pltpu.VMEM((hidden_n, width // 32), BF16)],
        compiler_params=streamed,
        cost_estimate=cost(256 * hidden_n * width, 4 * hidden_n * width),
    )(weight_codes[0], scales)
    received, others, weight = lax.optimization_barrier((received, others, weight))

    relay = pl.pallas_call(
        functools.partial(relay_kernel, slots, sources, side),
        out_shape=jax.ShapeDtypeStruct((side, main + main // 2, 128), BF16),
        in_specs=[SMEM, VMEM],
        out_specs=VMEM,
        scratch_shapes=[pltpu.VMEM((width, 256), F32)],
        compiler_params=params,
        cost_estimate=cost(8 * places * 256 * half, 4 * places * width),
    )(parity.reshape(1), received)
    relayed = exchange(relay, 0)

    hidden_grad, *scores = pl.pallas_call(
        functools.partial(hidden_kernel, slots, sources),
        out_shape=(
            jax.ShapeDtypeStruct((places, hidden_n), BF16),
            *[jax.ShapeDtypeStruct((sources // radix, 128), F32)] * radix,
        ),
        in_specs=[SMEM, HBM, HBM, HBM],
        out_specs=(VMEM,) + (VMEM,) * radix,
        scratch_shapes=[
            pltpu.VMEM((2 * places, half), BF16),
            pltpu.VMEM((hidden_n, width), F8),
            pltpu.VMEM((places, hidden_n), BF16),
            pltpu.VMEM((places, width), BF16),
            pltpu.SemaphoreType.DMA((2 + 2,)),
        ],
        compiler_params=streamed,
        cost_estimate=cost(4 * places * hidden_n * width, 2 * hidden_n * width),
    )(expert, received, weight, hidden)

    def passed_on(bit, scores):
        return [scores[0], shifted(scores[1], 1 << bit)]

    def regrouped(bit, scores):
        return pl.pallas_call(
            functools.partial(regroup_kernel, bit),
            out_shape=[jax.ShapeDtypeStruct((sources // radix, 128), F32)] * 2,
            in_specs=[VMEM] * 2,
            out_specs=[VMEM] * 2,
            compiler_params=params,
        )(*scores)

    scores = regrouped(0, passed_on(0, scores))
    scores = regrouped(1, passed_on(1, scores))
    scores = passed_on(2, scores)
    summed = pl.pallas_call(
        functools.partial(partial_kernel, side),
        out_shape=jax.ShapeDtypeStruct((main, subset), BF16),
        in_specs=[SMEM] + [VMEM] * (side + 1),
        out_specs=VMEM,
        scratch_shapes=[pltpu.VMEM((main, subset), F32)],
        compiler_params=params,
        cost_estimate=cost(2 * side * places * main * subset, 2 * side * places * (main + subset)),
    )(me.reshape(1), relayed, picked, *others)
    summed, scores = lax.optimization_barrier((summed, scores))
    returned = passed_on(3, regrouped(2, scores))
    terms = exchange(summed.reshape(side, main // side, subset), 1)
    weight_grad = jnp.sum(terms.astype(F32), axis=0)

    prob_grad = pl.pallas_call(
        functools.partial(prob_kernel, experts_n),
        out_shape=jax.ShapeDtypeStruct(routes_row.shape, F32),
        in_specs=[SMEM] + [VMEM] * (2 + radix),
        out_specs=VMEM,
        compiler_params=params,
    )(expert, routes_row, probs_row, *returned)
    return (
        hidden_grad.reshape(1, 1, slots, sources, hidden_n).transpose(0, 1, 3, 2, 4),
        weight_grad.reshape(1, main // side, subset),
        prob_grad.reshape(routes.shape),
    )


def solution(mesh):
    side = 8
    placed = (
        P(("expert", "replica"), None),
        P(("expert", "replica"), None),
        P(("expert", "replica"), None),
        P("expert", "replica", None, None, None),
        P("expert", None, None),
        P("expert", None, None),
        P("expert", None),
    )
    return jax.shard_map(
        functools.partial(per_device, side),
        mesh=mesh,
        in_specs=placed,
        out_specs=(
            P("expert", "replica", None, None, None),
            P("expert", "replica", None),
            P(("expert", "replica"), None),
        ),
        check_vma=False,
    )
```

```python
import functools

import jax
import jax.numpy as jnp
from jax import lax
from jax.experimental import pallas as pl
from jax.experimental.pallas import tpu as pltpu
from jax.sharding import PartitionSpec as P

F32 = jnp.float32
BF16 = jnp.bfloat16
F8 = jnp.float8_e5m2
BOTH = ("expert", "replica")
MIB = 1024 * 1024


def iota(shape, dim):
    return lax.broadcasted_iota(jnp.int32, shape, dim)


def ones_where(mask):
    return jnp.where(mask, 1.0, 0.0).astype(BF16)


def contract(a, b, da, db):
    return lax.dot_general(a, b, (((da,), (db,)), ((), ())), preferred_element_type=F32)


def slots_of(routes_row, experts_n):
    rows = routes_row.shape[1]
    named = iota((experts_n, rows), 0) == routes_row
    earlier = ones_where(iota((rows, rows), 0) < iota((rows, rows), 1))
    before = contract(ones_where(named), earlier, 1, 0)
    return named, jnp.sum(jnp.where(named, before, 0.0), axis=0, keepdims=True).astype(jnp.int32)


def pack_kernel(slots, experts_n, routes_ref, probs_ref, left_ref, right_ref, out_ref):
    routes = routes_ref[...]
    probs = probs_ref[...].astype(F32)
    _, slot = slots_of(routes, experts_n)
    target = routes * (2 * slots) + slot
    places = iota((out_ref.shape[0], routes.shape[1]), 0)
    left = jnp.where(places == target, probs, 0.0).astype(BF16)
    right = jnp.where(places == target + slots, probs, 0.0).astype(BF16)
    place = jnp.concatenate([left, right], axis=1)
    both = jnp.concatenate([left_ref[...], right_ref[...]], axis=0)
    out_ref[...] = contract(place, both, 1, 0).astype(BF16)


def pick_kernel(ids_ref, hidden_ref, out_ref):
    chosen = ones_where(iota((hidden_ref.shape[1], ids_ref.shape[1]), 0) == ids_ref[...])
    out_ref[...] = contract(hidden_ref[...], chosen, 1, 0).astype(BF16)


def relay_kernel(slots, sources, side, parity_ref, rows_ref, out_ref, total):
    half = rows_ref.shape[1]
    width = 2 * half
    piece = width // (side * side)
    main = side * piece
    rows = rows_ref.shape[0]
    lane = iota((rows, 256), 1)
    place = jnp.where(lane < 128, lane, 128 + (lane & 63))
    slot, source = place >> 4, place & 15
    step = half // 2
    for at in range(0, width, step):
        pick = ones_where(
            iota((rows, 256), 0) == source * (2 * slots) + (at // half) * slots + slot
        )
        block = rows_ref[:, at % half : at % half + step]
        total[at : at + step, :] = contract(block, pick, 0, 0)
    low = iota((piece, 128), 1) < 64

    def spread(where):
        for to in range(side):
            for part in range(side):
                at = where(to, part) * piece
                out_ref[to, part * piece : (part + 1) * piece, :] = total[
                    at : at + piece, 0:128
                ].astype(BF16)
            for part in range(side // 2):
                one = where(to, part) * piece
                two = where(to, part + side // 2) * piece
                both = jnp.where(
                    low, total[one : one + piece, 128:256], total[two : two + piece, 128:256]
                )
                out_ref[to, main + part * piece : main + (part + 1) * piece, :] = both.astype(BF16)

    @pl.when(parity_ref[0] == 0)
    def _():
        spread(lambda to, part: to * side + part)

    @pl.when(parity_ref[0] == 1)
    def _():
        spread(lambda to, part: part * side + to)


def weight_kernel(codes_ref, scales_ref, out_ref, factors):
    block = codes_ref.shape[1]
    groups = scales_ref.shape[0]
    step_n = pl.program_id(0)

    @pl.when(step_n == 0)
    def _():
        factors[...] = jnp.exp2((scales_ref[...] - 127).astype(F32)).T.astype(BF16)

    at = step_n * (block // 32) + (iota((groups, block), 1) >> 5)
    spread = contract(factors[...], ones_where(iota((groups, block), 0) == at), 1, 0)
    out_ref[...] = (codes_ref[...] * spread.astype(BF16)).astype(out_ref.dtype)


def hidden_kernel(slots, sources, me_ref, rows_hbm, weight_hbm, hidden_hbm, out_ref, *refs):
    score_refs, (rows_ref, weight_ref, hidden_ref, rows, sems) = refs[:-5], refs[-5:]
    radix = len(score_refs)
    places, hidden_n = out_ref.shape
    half = rows_ref.shape[1]
    blocks = sems.shape[0] - 2
    block = hidden_n // blocks
    loads = [pltpu.make_async_copy(rows_hbm, rows_ref, sems.at[blocks])]
    for n in range(blocks):
        part = pl.ds(n * block, block)
        loads.append(pltpu.make_async_copy(weight_hbm.at[part], weight_ref.at[part], sems.at[n]))
    loads.insert(2, pltpu.make_async_copy(hidden_hbm, hidden_ref, sems.at[blocks + 1]))
    for load in loads:
        load.start()
    rows_load, first_load, hidden_load, *rest = loads
    place = iota((places, rows_ref.shape[0]), 0)
    column = iota((places, rows_ref.shape[0]), 1)
    rows_load.wait()
    for part in range(2):
        pick = ones_where(column == (place & 15) * (2 * slots) + part * slots + (place >> 4))
        rows[:, part * half : (part + 1) * half] = contract(pick, rows_ref[...], 1, 0).astype(BF16)
    hidden_load.wait()
    score = jnp.zeros((places, 1), F32)
    for n, load in enumerate([first_load, *rest]):
        load.wait()
        part = slice(n * block, (n + 1) * block)
        through = contract(rows[...], weight_ref[part, :].astype(BF16), 1, 1)
        out_ref[:, part] = through.astype(BF16)
        score += jnp.sum(through * hidden_ref[:, part].astype(F32), axis=1, keepdims=True)
    by_slot = jnp.where(iota((places, 128), 1) == iota((places, 128), 0) >> 4, score, 0.0)
    rows_n = sources // radix
    ahead = iota((rows_n, places), 0) * radix + me_ref[0]
    for low, score_ref in enumerate(score_refs):
        to = (ahead + low) & 15
        by_source = jnp.where(to == iota((rows_n, places), 1) & 15, 1.0, 0.0)
        score_ref[...] = jnp.dot(
            by_source, by_slot, preferred_element_type=F32, precision=lax.Precision.HIGHEST
        )


def partial_kernel(side, me_ref, relayed_ref, *refs):
    picked, out_ref, total = refs[:-2], refs[-2], refs[-1]
    main = out_ref.shape[0]
    half = main // 2
    zeros = jnp.zeros((64, out_ref.shape[1]), BF16)
    total[...] = jnp.zeros_like(total)
    for distance in range(side):
        block = relayed_ref.at[lax.rem(me_ref[0] - distance + side, side)]
        own = picked[distance]
        total[...] += contract(block[:main, :], own[0:128, :], 1, 0)
        rest = own[128:192, :]
        tail = block[main : main + half, :]
        total[:half, :] += contract(tail, jnp.concatenate([rest, zeros], axis=0), 1, 0)
        total[half:, :] += contract(tail, jnp.concatenate([zeros, rest], axis=0), 1, 0)
    out_ref[...] = total[...].astype(BF16)


def keep_kernel(held_ref, out_ref):
    out_ref[...] = held_ref[...]


def with_bit(count, bit, value):
    return [j for j in range(count) if (j >> bit) & 1 == value]


def regroup_kernel(bit, *refs):
    count = 2 * refs[0].shape[0]
    for value in range(2):
        rows = []
        for j in with_bit(count, bit + 1, value):
            held = (j >> bit) & 1
            row = with_bit(count, bit, held).index(j)
            rows.append(refs[held][row : row + 1, :])
        refs[2 + value][...] = jnp.concatenate(rows, axis=0)


def prob_kernel(experts_n, me_ref, routes_ref, probs_ref, *refs):
    returned_refs, out_ref = refs[:-1], refs[-1]
    routes = routes_ref[...]
    _, slot = slots_of(routes, experts_n)
    named = (me_ref[0] - iota((experts_n, routes.shape[1]), 0)) & (experts_n - 1)
    mine = lax.dot_general(
        jnp.concatenate([ref[...] for ref in returned_refs], axis=0),
        jnp.where(named == routes, 1.0, 0.0),
        (((0,), (0,)), ((), ())),
        preferred_element_type=F32,
        precision=lax.Precision.HIGHEST,
    )
    score = jnp.sum(jnp.where(iota(mine.shape, 0) == slot, mine, 0.0), axis=0, keepdims=True)
    out_ref[...] = score / probs_ref[...].astype(F32)


VMEM = pl.BlockSpec(memory_space=pltpu.VMEM)
SMEM = pl.BlockSpec(memory_space=pltpu.SMEM)
HBM = pl.BlockSpec(memory_space=pltpu.HBM)


def cost(flops, moved):
    return pl.CostEstimate(flops=flops, bytes_accessed=moved, transcendentals=0)


def per_device(
    side, grad_out, route_probs, routes, hidden_saved, weight_codes, weight_scales, subset_ids
):
    experts_n = lax.axis_size("expert")
    width = grad_out.shape[1]
    sources, slots, hidden_n = hidden_saved.shape[2:]
    subset = subset_ids.shape[1]
    places = sources * slots
    half = width // 2
    main = width // side
    replica = lax.axis_index("replica")
    expert = lax.axis_index("expert").reshape(1)
    parity = lax.axis_index("expert") % 2
    radix = 2
    me = jnp.where(parity == 0, replica // side, replica % side).astype(jnp.int32)
    params = pltpu.CompilerParams(vmem_limit_bytes=16 * MIB)
    streamed = pltpu.CompilerParams(vmem_limit_bytes=56 * MIB)

    def at(e, y, z):
        return e * side * side + (y % side) * side + z % side

    lines = [
        [[at(e, b, a) if e % 2 == turn else at(e, a, b) for b in range(side)] for e in range(experts_n) for a in range(side)]
        for turn in (0, 1)
    ]

    def moves(by):
        return [
            (at(e, y, z), at(e, y + by, z) if e % 2 == 0 else at(e, y, z + by))
            for e in range(experts_n)
            for y in range(side)
            for z in range(side)
        ]

    def exchange(x, turn):
        return lax.all_to_all(
            x, BOTH, split_axis=0, concat_axis=0, tiled=True, axis_index_groups=lines[turn]
        )

    def shifted(x, by):
        return lax.ppermute(x, "expert", [(e, (e + by) % experts_n) for e in range(experts_n)])

    routes_row = routes.reshape(1, -1)
    probs_row = route_probs.reshape(1, -1)
    hidden = hidden_saved.transpose(0, 1, 3, 2, 4).reshape(places, hidden_n)

    chunks = 2
    tokens = grad_out.shape[0]
    packed = pl.pallas_call(
        functools.partial(pack_kernel, slots, experts_n),
        grid=(chunks,),
        out_shape=jax.ShapeDtypeStruct((2 * places, half), BF16),
        in_specs=[
            pl.BlockSpec((1, tokens), lambda i: (0, 0)),
            pl.BlockSpec((1, tokens), lambda i: (0, 0)),
            pl.BlockSpec((tokens, half // chunks), lambda i: (0, i)),
            pl.BlockSpec((tokens, half // chunks), lambda i: (0, i + chunks)),
        ],
        out_specs=pl.BlockSpec((2 * places, half // chunks), lambda i: (0, i)),
        compiler_params=pltpu.CompilerParams(vmem_limit_bytes=63 * MIB),
        cost_estimate=cost(8 * places * 128 * half, 3 * places * width),
    )(routes_row, probs_row, grad_out, grad_out)
    received = lax.all_to_all(
        packed.reshape(experts_n, 2 * slots, half), "expert", split_axis=0, concat_axis=0, tiled=True
    ).reshape(2 * places, half)

    ids, scales, _ = lax.optimization_barrier((subset_ids, weight_scales[0].T, packed))
    picked = pl.pallas_call(
        pick_kernel,
        out_shape=jax.ShapeDtypeStruct((places, subset), BF16),
        in_specs=[VMEM] * 2,
        out_specs=VMEM,
        compiler_params=params,
        cost_estimate=cost(2 * places * hidden_n * subset, 2 * places * hidden_n),
    )(ids, hidden)
    others = [lax.ppermute(picked, BOTH, moves(by)) for by in range(1, side)]
    blocks = 4
    weight = pl.pallas_call(
        weight_kernel,
        grid=(blocks,),
        out_shape=jax.ShapeDtypeStruct((hidden_n, width), F8),
        in_specs=[
            pl.BlockSpec((hidden_n, width // blocks), lambda i: (0, i)),
            pl.BlockSpec((width // 32, hidden_n), lambda i: (0, 0)),
        ],
        out_specs=pl.BlockSpec((hidden_n, width // blocks), lambda i: (0, i)),
        scratch_shapes=[pltpu.VMEM((hidden_n, width // 32), BF16)],
        compiler_params=streamed,
        cost_estimate=cost(256 * hidden_n * width, 4 * hidden_n * width),
    )(weight_codes[0], scales)
    received, others, weight = lax.optimization_barrier((received, others, weight))

    relay = pl.pallas_call(
        functools.partial(relay_kernel, slots, sources, side),
        out_shape=jax.ShapeDtypeStruct((side, main + main // 2, 128), BF16),
        in_specs=[SMEM, VMEM],
        out_specs=VMEM,
        scratch_shapes=[pltpu.VMEM((width, 256), F32)],
        compiler_params=params,
        cost_estimate=cost(8 * places * 256 * half, 4 * places * width),
    )(parity.reshape(1), received)
    relayed = exchange(relay, 0)

    hidden_grad, *scores = pl.pallas_call(
        functools.partial(hidden_kernel, slots, sources),
        out_shape=(
            jax.ShapeDtypeStruct((places, hidden_n), BF16),
            *[jax.ShapeDtypeStruct((sources // radix, 128), F32)] * radix,
        ),
        in_specs=[SMEM, HBM, HBM, HBM],
        out_specs=(VMEM,) + (VMEM,) * radix,
        scratch_shapes=[
            pltpu.VMEM((2 * places, half), BF16),
            pltpu.VMEM((hidden_n, width), F8),
            pltpu.VMEM((places, hidden_n), BF16),
            pltpu.VMEM((places, width), BF16),
            pltpu.SemaphoreType.DMA((2 + 2,)),
        ],
        compiler_params=streamed,
        cost_estimate=cost(4 * places * hidden_n * width, 2 * hidden_n * width),
    )(expert, received, weight, hidden)

    def passed_on(bit, scores):
        return [scores[0], shifted(scores[1], 1 << bit)]

    def regrouped(bit, scores):
        return pl.pallas_call(
            functools.partial(regroup_kernel, bit),
            out_shape=[jax.ShapeDtypeStruct((sources // radix, 128), F32)] * 2,
            in_specs=[VMEM] * 2,
            out_specs=[VMEM] * 2,
            compiler_params=params,
        )(*scores)

    kept = pl.pallas_call(
        keep_kernel,
        out_shape=jax.ShapeDtypeStruct(scores[0].shape, F32),
        in_specs=[VMEM],
        out_specs=VMEM,
        compiler_params=params,
    )(scores[0])
    scores = regrouped(0, [kept, shifted(scores[1], 1)])
    scores = regrouped(1, passed_on(1, scores))
    scores = passed_on(2, scores)
    summed = pl.pallas_call(
        functools.partial(partial_kernel, side),
        out_shape=jax.ShapeDtypeStruct((main, subset), BF16),
        in_specs=[SMEM] + [VMEM] * (side + 1),
        out_specs=VMEM,
        scratch_shapes=[pltpu.VMEM((main, subset), F32)],
        compiler_params=params,
        cost_estimate=cost(2 * side * places * main * subset, 2 * side * places * (main + subset)),
    )(me.reshape(1), relayed, picked, *others)
    summed, scores = lax.optimization_barrier((summed, scores))
    returned = passed_on(3, regrouped(2, scores))
    terms = exchange(summed.reshape(side, main // side, subset), 1)
    weight_grad = jnp.sum(terms.astype(F32), axis=0)

    prob_grad = pl.pallas_call(
        functools.partial(prob_kernel, experts_n),
        out_shape=jax.ShapeDtypeStruct(routes_row.shape, F32),
        in_specs=[SMEM] + [VMEM] * (2 + radix),
        out_specs=VMEM,
        compiler_params=params,
    )(expert, routes_row, probs_row, *returned)
    return (
        hidden_grad.reshape(1, 1, slots, sources, hidden_n).transpose(0, 1, 3, 2, 4),
        weight_grad.reshape(1, main // side, subset),
        prob_grad.reshape(routes.shape),
    )


def solution(mesh):
    side = 8
    placed = (
        P(("expert", "replica"), None),
        P(("expert", "replica"), None),
        P(("expert", "replica"), None),
        P("expert", "replica", None, None, None),
        P("expert", None, None),
        P("expert", None, None),
        P("expert", None),
    )
    return jax.shard_map(
        functools.partial(per_device, side),
        mesh=mesh,
        in_specs=placed,
        out_specs=(
            P("expert", "replica", None, None, None),
            P("expert", "replica", None),
            P(("expert", "replica"), None),
        ),
        check_vma=False,
    )
```
